32 devices in a mesh: groups: 2 (over y), expert: 8 (over z, core), dp: 2 (over x), node: 1.
Axes of the slice: x: 2, y: 2, z: 4, core: 2. Of those that a mesh axis runs over, the one named last changes fastest.
Arguments:
- grad_out: bfloat16 [4096, 4096], P(('groups', 'expert', 'dp', 'node')), parts along dimension 0, may hold values from -4 to 4
- routes: int32 [4096, 4], P(('groups', 'expert', 'dp', 'node')), parts along dimension 0, may hold values from 0 to 7, all different within a row; in each aligned block of 128 rows (0 to 127, 128 to 255, ...) at most 68 rows name the same one
- gates: bfloat16 [4096, 4], P(('groups', 'expert', 'dp', 'node')), parts along dimension 0, may hold values from 0.049804688 to 1
- gate_pre: bfloat16 [16, 2, 8, 68, 768], P(('groups', 'expert'), 'dp', None, None, 'node'), parts along dimension 0, may hold values from -6 to 6
- up_pre: bfloat16 [16, 2, 8, 68, 768], P(('groups', 'expert'), 'dp', None, None, 'node'), parts along dimension 0, may hold values from -6 to 6
- w_down: bfloat16 [8, 4096, 768], P('expert', 'dp', 'node'), may hold values from -0.21875 to 0.21875
Outputs:
- d_gates: float32 [4096, 4], P(('groups', 'expert', 'dp', 'node')), parts along dimension 0
- d_gate_pre: bfloat16 [16, 2, 8, 68, 768], P(('groups', 'expert'), 'dp', None, None, 'node'), parts along dimension 0
- d_up_pre: bfloat16 [16, 2, 8, 68, 768], P(('groups', 'expert'), 'dp', None, None, 'node'), parts along dimension 0
- d_w_down: bfloat16 [16, 4096, 768], P(('groups', 'expert'), 'dp', 'node'), parts along dimension 0
The draws below stay inside these ranges and needn't reach their ends.
There are 2 independent parts, one for each index of `groups`. The reference program is written for one: setup_inputs(seed, part) draws one part's arguments, and reference() takes and returns one part's arrays. A program takes and returns all parts, laid end to end along the dimension named above; an argument that names none is the same for every part. Nothing has to cross between parts.
Inputs may be any that keep to these rules, and one draw needn't show every extreme that they name: `routes`: in the rows of one device no expert is named by more than 68 entries, a bound that some block reaches of them; the 4 experts of a token differ.
All inputs are finite; a program needn't handle non-finite values.
Results may differ from the reference program's by a relative error of at most 0.017.
Values may be sent and summed in bfloat16 or wider, within the bound.
A program may use at most 128 MiB of HBM per device.

```python
import math
import jax
import jax.numpy as jnp
import numpy as np
from jax import lax

D = 4096
H = 768
TOPK = 4
TOK_DEV = 128
EXPERTS = 8
SRC = 8
CAP = 68
TOKENS = 2048
N_DP = 2
N_NODE = 1


def steps_of(rng, extent, split, least, largest):
    gain, own = 1.0, jax.random.fold_in(rng, 6)
    for axis_at, shards_of in split:
        heights = jnp.exp(jax.random.uniform(jax.random.fold_in(own, axis_at), (shards_of,), jnp.float32, least / len(split), largest / len(split)))
        gain = gain * jnp.repeat(heights, extent[axis_at] // shards_of).reshape([-1 if axis == axis_at else 1 for axis in range(len(extent))])
    return gain


def shared_out(key, own, number, rows, count, top, bound, lean):
    sequence = jax.random.permutation(key, count)
    heavy_load, common = shares(count, rows * top, bound, lean, True), shares(count, rows * top, bound, lean, False)
    places = jnp.arange(count)

    def named(lengths, turn):
        used = int((lengths > 0).sum())
        fixed = max(1, used // 4)
        shifted = fixed + (places - fixed + turn * (used - fixed)) % max(1, count - fixed)
        return jnp.zeros((count,), jnp.int32).at[sequence[jnp.where(places < fixed, places, shifted)]].set(jnp.asarray(lengths, jnp.int32))

    lengths = jnp.where(number % 4 == 0, named(heavy_load, number // 4), named(common, number - number // 4 - 1))
    mixed = jax.random.permutation(jax.random.fold_in(own, 3), count)
    source_of, sink = mixed[0:count // 2 * 2:2], mixed[1:count // 2 * 2:2]
    slack = jnp.minimum(lengths[source_of] - 1, bound - lengths[sink]) // 2
    slack = jnp.where((source_of == sequence[0]) | (sink == sequence[0]) | (lengths[sink] == 0), 0, jnp.maximum(slack, 0))
    shifted = jax.random.randint(jax.random.fold_in(own, 4), (count // 2,), 0, 1 << 20) % (slack + 1)
    lengths = lengths.at[source_of].add(-shifted).at[sink].add(shifted)
    labels = jnp.searchsorted(jnp.cumsum(lengths), jnp.arange(rows * top), side="right").astype(jnp.int32)
    grid = labels.reshape(top, rows).T
    grid = grid[jax.random.permutation(jax.random.fold_in(own, 1), rows)]
    turn = jax.random.randint(jax.random.fold_in(own, 2), (rows, 1), 0, top)
    return jnp.take_along_axis(grid, (jnp.arange(top)[None, :] + turn) % top, axis=1)


def shares(number_of, total, limit, skew, full):
    portions = [(1 << 20) // math.isqrt(standing ** skew) + 1 for standing in range(1, number_of + 1)]
    largest = limit if full else min(limit, max(-(-total // number_of), total * portions[0] // sum(portions)))
    least = 1 if total - largest >= number_of - 1 else 0
    counts, rest = [largest] + [least] * (number_of - 1), total - largest - least * (number_of - 1)
    while rest > 0:
        movable = [i for i in range(1, number_of) if counts[i] < largest] or [i for i in range(1, number_of) if counts[i] < limit]
        pool, budget = sum([portions[i] for i in movable]), rest
        for i in movable:
            extra = min(limit - counts[i], max(1, budget * portions[i] // pool), rest)
            counts[i] = counts[i] + extra
            rest = rest - extra
    return np.array(counts)


def centred(own_key, extent, scale, most, pieces=(), kind=jnp.bfloat16):
    values = scale * jax.random.normal(own_key, extent, jnp.float32)
    if pieces:
        values = values * steps_of(own_key, extent, pieces, -0.22, 0.18)
    return jnp.clip(values, -most, most).astype(kind)


def setup_inputs(seed: int = 0, part: int = 0) -> dict:
    keys = jax.random.split(jax.random.key(seed), 7)
    part_keys = jax.random.split(jax.random.fold_in(keys[6], part), 7)
    grad_out = centred(part_keys[0], (TOKENS, D), 0.25, 4.0, ((0, 16),))
    routes_keys = jax.random.split(jax.random.fold_in(part_keys[1], 1), TOKENS // TOK_DEV)
    routes_turns = jax.random.permutation(jax.random.fold_in(part_keys[1], 3), TOKENS // TOK_DEV)
    routes = jax.vmap(lambda own, number: shared_out(jax.random.fold_in(part_keys[1], 2), own, number, TOK_DEV, EXPERTS, TOPK, CAP, 1))(routes_keys, routes_turns).reshape((TOKENS, TOPK))
    gates = jnp.clip(jnp.exp(math.log(1.0) - 2.9996462 * jax.random.uniform(part_keys[2], (TOKENS, TOPK), jnp.float32) ** steps_of(part_keys[2], (TOKENS, TOPK), ((0, 16),), -0.2, 0.2)), 0.049804688, 1.0).astype(jnp.bfloat16)
    gate_pre = centred(part_keys[3], (EXPERTS, N_DP, SRC, CAP, H), 1.0, 6.0, ((0, 8), (1, 2)))
    up_pre = centred(part_keys[4], (EXPERTS, N_DP, SRC, CAP, H), 1.0, 6.0, ((0, 8), (1, 2)))
    w_down = centred(keys[5], (EXPERTS, D, H), H ** -0.5, 0.21875, ((0, 8), (1, 2)))
    return {"grad_out": grad_out, "routes": routes, "gates": gates, "gate_pre": gate_pre, "up_pre": up_pre, "w_down": w_down}


def reference(grad_out, routes, gates, gate_pre, up_pre, w_down):
    count = TOK_DEV * TOPK
    blocks = TOKENS // TOK_DEV
    slots = N_DP * SRC * CAP
    flat_routes = routes.reshape(blocks, count)
    member = (flat_routes[:, :, None] == jnp.arange(EXPERTS, dtype=jnp.int32)[None, None, :]).astype(jnp.int32)
    rank = jnp.sum(jnp.cumsum(member, axis=1) * member, axis=2) - 1
    block_ids = jnp.arange(blocks, dtype=jnp.int32)
    owner_src = block_ids // (N_DP * N_NODE)
    dp_index = (block_ids // N_NODE) % N_DP
    node_index = block_ids % N_NODE
    source = owner_src * N_NODE + node_index
    position = (dp_index * SRC + source)[:, None] * CAP + rank
    flat_index = (flat_routes * slots + position).reshape(-1).astype(jnp.int32)
    token_ids = (jnp.arange(blocks * count, dtype=jnp.int32) // TOPK).astype(jnp.int32)
    slot_token = jnp.full((EXPERTS * slots,), TOKENS, jnp.int32).at[flat_index].set(token_ids).reshape(EXPERTS, slots)
    slot_gate = jnp.zeros((EXPERTS * slots,), jnp.float32).at[flat_index].set(gates.reshape(-1).astype(jnp.float32)).reshape(EXPERTS, slots)

    def one_expert(inputs):
        tok_index, gate_col, pre_gate, pre_up, weight = inputs
        rows = jnp.take(grad_out, tok_index, axis=0, mode="fill", fill_value=0)
        pre_a = pre_gate.reshape(slots, H).astype(jnp.float32)
        pre_u = pre_up.reshape(slots, H).astype(jnp.float32)
        grad_h = jnp.dot(rows, weight, preferred_element_type=jnp.float32)
        sig = jax.nn.sigmoid(pre_a)
        act = pre_a * sig
        hact = act * pre_u
        score = jnp.sum(grad_h * hact, axis=1)
        d_act = gate_col[:, None] * grad_h
        d_a = (d_act * pre_u * sig * (1.0 + pre_a * (1.0 - sig))).astype(jnp.bfloat16)
        d_u = (d_act * act).astype(jnp.bfloat16)
        weighted = (gate_col[:, None] * hact).astype(jnp.bfloat16)
        parts = jnp.einsum("pmd,pmh->pdh", rows.reshape(N_DP, SRC * CAP, D).astype(jnp.float32), weighted.reshape(N_DP, SRC * CAP, H).astype(jnp.float32))
        parts = lax.optimization_barrier(parts.astype(jnp.bfloat16))
        grad_w = jnp.sum(parts.astype(jnp.float32), axis=0).astype(jnp.bfloat16)
        return score, d_a.reshape(N_DP, SRC, CAP, H), d_u.reshape(N_DP, SRC, CAP, H), grad_w

    scores, d_gate_pre, d_up_pre, d_w_down = lax.map(one_expert, (slot_token, slot_gate, gate_pre, up_pre, w_down))
    d_gates = scores.reshape(-1)[flat_index].reshape(TOKENS, TOPK)
    return d_gates, d_gate_pre, d_up_pre, d_w_down
```

```python
import jax
import jax.numpy as jnp
from jax import lax
from jax.experimental import pallas as pl
from jax.experimental.pallas import tpu as pltpu
from jax.sharding import PartitionSpec as P


PAD = 80
TILE = 512


def whole_kernel(
    meta_ref, gout, gpre, upre, wdn, dg_ref, da_ref, du_ref, dw_out,
    tok, wv, rows, own, dhs, dhr, wall, acc, dwv, mb, rk, gt, scs, scr,
    loc, x_sem, m_send, m_recv, z_up, z_dn, z_recv, c_send, c_recv, d_send, d_recv,
    w_send, w_recv, s_send, s_recv, o_sem,
):
    half = wv.shape[0]
    cap = gpre.shape[3]
    e = lax.axis_index("expert")
    x = lax.axis_index("dp")
    z, c = e // 2, e % 2
    ox = 1 - x
    sib = 2 * z + 1 - c
    hid = wv.shape[1]

    def remote(src, dst, ss, rs, ee, xx):
        return pltpu.make_async_remote_copy(
            src_ref=src, dst_ref=dst, send_sem=ss, recv_sem=rs,
            device_id={"expert": ee, "dp": xx}, device_id_type=pl.DeviceIdType.MESH,
        )

    def order(k):
        inner = jnp.where(k == 0, 1, jnp.where(k == 1, 0, k))
        low = jnp.where((z == 1) | (z == 2), inner, k)
        return jnp.where(z < 2, low, 3 - low)

    mine = gout.at[:, pl.ds(pl.multiple_of(x * half, 128), half)]
    other = gout.at[:, pl.ds(pl.multiple_of(ox * half, 128), half)]
    tok_copy = pltpu.make_async_copy(mine, tok.at[e, 0], loc.at[0])
    w_copy = pltpu.make_async_copy(wdn.at[0], wv, loc.at[1])
    tok_copy.start()
    w_copy.start()
    barrier = pltpu.get_barrier_semaphore()
    peers = [((e + d) % 8, x, 0, e, (e + d) % 8) for d in range(1, 8)]
    peers += [((e + d) % 8, ox, 1, e + 8, (e + d) % 8 + 8) for d in range(8)]
    for ee, xx, _, _, _ in peers:
        pl.semaphore_signal(
            barrier, inc=1, device_id={"expert": ee, "dp": xx},
            device_id_type=pl.DeviceIdType.MESH,
        )
    mb[e] = meta_ref[...]
    wall[:, 0:2 * PAD, :] = jnp.zeros((4, 2 * PAD, hid), jnp.bfloat16)
    tok_copy.wait()
    pl.semaphore_wait(barrier, 15)

    def meta_copy(i):
        ee, xx, q, slot, _ = peers[i]
        return remote(meta_ref, mb.at[slot], m_send.at[i], m_recv.at[slot], ee, xx)

    for i in range(15):
        meta_copy(i).start()
    x_copy = remote(other, tok.at[e, 1], x_sem.at[0], x_sem.at[1], e, ox)
    x_copy.start()

    def up(zp, q):
        t = tok.at[2 * zp + c, q]
        return remote(t, t, z_up.at[zp, q], z_recv.at[zp, q], e + 2, x)

    def down(zp, q):
        t = tok.at[2 * zp + c, q]
        return remote(t, t, z_dn.at[zp, q], z_recv.at[zp, q], e - 2, x)

    def across(zp, q):
        t = tok.at[2 * zp + c, q]
        return remote(t, t, c_send.at[zp, q], c_recv.at[zp, q], sib, x)

    def arrived(zp, q):
        t = tok.at[2 * zp + c, q]
        remote(t, t, z_up.at[zp, q], z_recv.at[zp, q], e, ox).wait_recv()

    def sibling(zp, q):
        t = tok.at[2 * zp + 1 - c, q]
        remote(t, t, c_send.at[zp, q], c_recv.at[zp, q], sib, x).wait_recv()

    def forward(zp, q):
        @pl.when((zp <= z) & (z < 3))
        def _():
            up(zp, q).start()

        @pl.when((zp >= z) & (z > 0))
        def _():
            down(zp, q).start()

        across(zp, q).start()

    forward(z, 0)

    for i in range(15):
        ee, xx, q, _, slot = peers[i]
        remote(meta_ref, mb.at[slot], m_send.at[i], m_recv.at[slot], ee, xx).wait_recv()

    named = (mb[:, 0:4, :] == e.astype(jnp.float32)).astype(jnp.float32)
    hit = jnp.sum(named, axis=1)
    gt[...] = jnp.sum(named * mb[:, 4:8, :], axis=1)
    before = (
        lax.broadcasted_iota(jnp.int32, (128, 128), 0)
        < lax.broadcasted_iota(jnp.int32, (128, 128), 1)
    )
    rank = jnp.dot(
        hit.astype(jnp.bfloat16), before.astype(jnp.float32).astype(jnp.bfloat16),
        preferred_element_type=jnp.float32,
    )
    rk[...] = jnp.where(hit > 0.5, rank, -1.0)
    slot_id = lax.broadcasted_iota(jnp.int32, (PAD, 128), 0).astype(jnp.float32)

    def placer(b):
        return (slot_id == rk[pl.ds(b, 1), :]).astype(jnp.float32)

    def w_copy_out(zp):
        return remote(
            wall.at[zp, 0:2 * PAD], wall.at[zp, 2 * PAD:4 * PAD],
            w_send.at[zp], w_recv.at[zp], e, ox,
        )

    @pl.loop(0, 4)
    def _(k):
        zp = order(k)
        for cc in range(2):
            s = 2 * zp + cc
            place = placer(s)
            gate = jnp.sum(place * gt[pl.ds(s, 1), :], axis=1, keepdims=True)[0:cap]
            a = gpre[0, 0, s].astype(jnp.float32)
            u = upre[0, 0, s].astype(jnp.float32)
            wall[zp, cc * PAD:cc * PAD + cap, :] = (
                gate * (a * jax.nn.sigmoid(a) * u)
            ).astype(jnp.bfloat16)
        w_copy_out(zp).start()

    acc[...] = jnp.zeros_like(acc)
    w_copy.wait()

    def dh_copy(zp):
        return remote(dhs.at[zp], dhr.at[zp], d_send.at[zp], d_recv.at[zp], e, ox)

    def score_copy(s):
        return remote(scs.at[s], scr.at[e], s_send.at[s], s_recv.at[e], s, x)

    def finish(zp, last):
        w_copy_out(zp).wait_recv()

        @pl.loop(0, half // TILE)
        def _(t):
            at = pl.ds(pl.multiple_of(t * TILE, TILE), TILE)
            total = acc[at, :] + lax.dot_general(
                rows[:, at], wall[zp], (((0,), (0,)), ((), ())),
                preferred_element_type=jnp.float32,
            )
            if last:
                dwv[at, :] = total.astype(jnp.bfloat16)
                pltpu.make_async_copy(dwv.at[at, :], dw_out.at[0, at, :], o_sem.at[t]).start()
            else:
                acc[at, :] = total

        dh_copy(zp).wait_recv()
        for cc in range(2):
            s = 2 * zp + cc
            place = placer(s)
            gate = jnp.sum(place * gt[pl.ds(s, 1), :], axis=1, keepdims=True)[0:cap]
            a = gpre[0, 0, s].astype(jnp.float32)
            u = upre[0, 0, s].astype(jnp.float32)
            dh = (own[cc] + dhr[zp, cc * PAD:(cc + 1) * PAD, :].astype(jnp.float32))
            dh = dh[0:cap]
            sig = jax.nn.sigmoid(a)
            act = a * sig
            score = jnp.sum(dh * (act * u), axis=1, keepdims=True)
            d_act = gate * dh
            da_ref[0, 0, s] = (d_act * u * sig * (1.0 + a * (1.0 - sig))).astype(jnp.bfloat16)
            du_ref[0, 0, s] = (d_act * act).astype(jnp.bfloat16)
            by_token = jnp.sum(place[0:cap] * score, axis=0, keepdims=True)
            full = jnp.broadcast_to(by_token, (8, 128))

            @pl.when(s == e)
            def _():
                scr[e] = full

            @pl.when(s != e)
            def _():
                scs[s] = full
                score_copy(s).start()

    @pl.loop(0, 4)
    def _(k):
        zp = order(k)

        @pl.when(k > 0)
        def _():
            arrived(zp, 0)
            forward(zp, 0)
            finish(order(k - 1), False)
            arrived(zp, 1)

        @pl.when(k == 0)
        def _():
            x_copy.wait_recv()

        forward(zp, 1)
        sibling(zp, 0)
        sibling(zp, 1)
        for q in (1, 0):
            for cc in range(2):
                s = 2 * zp + cc
                j = (q * 2 + cc) * PAD
                rows[j:j + PAD, :] = jnp.dot(
                    placer(q * 8 + s).astype(jnp.bfloat16), tok[s, q],
                    preferred_element_type=jnp.float32,
                ).astype(jnp.bfloat16)
            part = jnp.dot(
                rows[q * 2 * PAD:(q + 1) * 2 * PAD, :], wv[...],
                preferred_element_type=jnp.float32,
            )
            if q == 1:
                dhs[zp] = part.astype(jnp.bfloat16)
                dh_copy(zp).start()
            else:
                own[...] = part.reshape(2, PAD, hid)

    finish(order(3), True)

    for d in range(1, 8):
        s = (e + d) % 8
        remote(scs.at[s], scr.at[s], s_send.at[s], s_recv.at[s], s, x).wait_recv()
    routes = meta_ref[0:4, :]
    total = jnp.zeros((4, 128), jnp.float32)
    for i in range(8):
        total += jnp.where(routes == float(i), scr[i, 0:1, :], 0.0)
    dg_ref[...] = total

    x_copy.wait_send()
    for i in range(15):
        meta_copy(i).wait_send()
    for zp in range(4):
        for q in range(2):
            @pl.when((zp <= z) & (z < 3))
            def _():
                up(zp, q).wait_send()

            @pl.when((zp >= z) & (z > 0))
            def _():
                down(zp, q).wait_send()

            across(zp, q).wait_send()
        dh_copy(zp).wait_send()
        w_copy_out(zp).wait_send()
    for d in range(1, 8):
        score_copy((e + d) % 8).wait_send()
    for t in range(half // TILE):
        at = pl.ds(t * TILE, TILE)
        pltpu.make_async_copy(dwv.at[at, :], dw_out.at[0, at, :], o_sem.at[t]).wait()


def local_kernel(grad_out, routes, gates, gate_pre, up_pre, w_down):
    half, hid = w_down.shape[1], w_down.shape[2]
    meta = jnp.concatenate(
        [routes.astype(jnp.float32), gates.astype(jnp.float32)], axis=1
    ).T
    vmem = pl.BlockSpec(memory_space=pltpu.VMEM)
    hbm = pl.BlockSpec(memory_space=pl.ANY)
    dma = pltpu.SemaphoreType.DMA
    bf, f4 = jnp.bfloat16, jnp.float32
    dg, d_a, d_u, d_w = pl.pallas_call(
        whole_kernel,
        out_shape=(
            jax.ShapeDtypeStruct((4, 128), f4),
            jax.ShapeDtypeStruct(gate_pre.shape, bf),
            jax.ShapeDtypeStruct(up_pre.shape, bf),
            jax.ShapeDtypeStruct(w_down.shape, bf),
        ),
        in_specs=[vmem, hbm, vmem, vmem, hbm],
        out_specs=(vmem, vmem, vmem, hbm),
        scratch_shapes=[
            pltpu.VMEM((8, 2, 128, half), bf),
            pltpu.VMEM((half, hid), bf),
            pltpu.VMEM((4 * PAD, half), bf),
            pltpu.VMEM((2, PAD, hid), f4),
            pltpu.VMEM((4, 2 * PAD, hid), bf),
            pltpu.VMEM((4, 2 * PAD, hid), bf),
            pltpu.VMEM((4, 4 * PAD, hid), bf),
            pltpu.VMEM((half, hid), f4),
            pltpu.VMEM((half, hid), bf),
            pltpu.VMEM((16, 8, 128), f4),
            pltpu.VMEM((16, 128), f4),
            pltpu.VMEM((16, 128), f4),
            pltpu.VMEM((8, 8, 128), f4),
            pltpu.VMEM((8, 8, 128), f4),
            dma((2,)), dma((2,)), dma((15,)), dma((16,)),
            dma((4, 2)), dma((4, 2)), dma((4, 2)), dma((4, 2)), dma((4, 2)),
            dma((4,)), dma((4,)), dma((4,)), dma((4,)),
            dma((8,)), dma((8,)), dma((half // TILE,)),
        ],
        compiler_params=pltpu.CompilerParams(
            collective_id=0, has_side_effects=True, vmem_limit_bytes=56 * 1024 * 1024
        ),
    )(meta, grad_out, gate_pre, up_pre, w_down)
    return (dg.T, d_a, d_u, d_w)


def local(grad_out, routes, gates, gate_pre, up_pre, w_down):
    tok_rows, width = grad_out.shape
    topk = routes.shape[1]
    sources = gate_pre.shape[2]
    capacity = gate_pre.shape[3]
    hidden = gate_pre.shape[4]
    experts = lax.axis_size("expert")
    node_count = lax.axis_size("node")
    count = tok_rows * topk
    slot_count = sources * capacity
    flat_routes = routes.reshape(count)
    member = (flat_routes[:, None] == jnp.arange(experts, dtype=jnp.int32)[None, :]).astype(
        jnp.int32
    )
    rank = jnp.sum(jnp.cumsum(member, axis=0) * member, axis=1) - 1
    slot_of = flat_routes * capacity + rank
    placer = jnp.arange(experts * capacity, dtype=jnp.int32)[:, None] == slot_of[None, :]
    placer_f = placer.astype(jnp.float32)
    by_token = jnp.sum(
        placer.reshape(experts * capacity, tok_rows, topk).astype(jnp.int32), axis=2
    ).astype(jnp.bfloat16)
    send_rows = (
        jnp.dot(by_token, grad_out, preferred_element_type=jnp.float32)
        .astype(jnp.bfloat16)
        .reshape(experts, capacity, width)
    )
    send_gates = (
        jnp.dot(placer_f, gates.reshape(count).astype(jnp.float32), precision=lax.Precision.HIGHEST)
        .astype(jnp.bfloat16)
        .reshape(experts, capacity)
    )
    pair_rows, pair_gates = (
        lax.all_gather(send_rows[None], "node", axis=0, tiled=True),
        lax.all_gather(send_gates[None], "node", axis=0, tiled=True),
    )
    recv_rows, recv_gates = (
        lax.all_to_all(pair_rows, "expert", split_axis=1, concat_axis=0, tiled=True),
        lax.all_to_all(pair_gates, "expert", split_axis=1, concat_axis=0, tiled=True),
    )
    rows = recv_rows.reshape(slot_count, width)
    gate_col = recv_gates.reshape(slot_count).astype(jnp.float32)
    pre_a = gate_pre.reshape(slot_count, hidden).astype(jnp.float32)
    pre_u = up_pre.reshape(slot_count, hidden).astype(jnp.float32)
    columns = rows
    grad_h = jnp.dot(
        columns,
        lax.all_gather(w_down, "dp", axis=1, tiled=True)[0],
        preferred_element_type=jnp.float32,
    )
    sig = jax.nn.sigmoid(pre_a)
    act = pre_a * sig
    hact = act * pre_u
    partial_score = jnp.sum(grad_h * hact, axis=1)
    d_act = gate_col[:, None] * grad_h
    d_a = (
        (d_act * pre_u * sig * (1.0 + pre_a * (1.0 - sig)))
        .astype(jnp.bfloat16)
        .reshape(gate_pre.shape)
    )
    d_u = (d_act * act).astype(jnp.bfloat16).reshape(up_pre.shape)
    weighted = (gate_col[:, None] * hact).astype(jnp.bfloat16)
    columns = rows
    grad_w = lax.psum_scatter(
        lax.dot_general(
            columns, weighted, (((0,), (0,)), ((), ())), preferred_element_type=jnp.float32
        ).astype(jnp.bfloat16),
        "dp",
        scatter_dimension=0,
        tiled=True,
    )
    d_w = grad_w[None]
    returned = lax.all_to_all(
        partial_score.reshape(sources, 1, capacity),
        ("expert", "node"),
        split_axis=0,
        concat_axis=1,
        tiled=True,
    )
    summed = jnp.sum(returned.reshape(experts, node_count, capacity), axis=1).reshape(
        experts * capacity
    )
    d_gates = jnp.dot(summed, placer_f, precision=lax.Precision.HIGHEST).reshape(tok_rows, topk)
    return (d_gates, d_a, d_u, d_w)


def solution(mesh):
    placed = (
        P(("groups", "expert", "dp", "node"), None),
        P(("groups", "expert", "dp", "node"), None),
        P(("groups", "expert", "dp", "node"), None),
        P(("groups", "expert"), "dp", None, None, "node"),
        P(("groups", "expert"), "dp", None, None, "node"),
        P("expert", "dp", "node"),
    )
    sizes = dict(mesh.shape)
    small = (sizes["expert"], sizes["dp"], sizes["node"]) == (8, 2, 1)
    return jax.shard_map(
        local_kernel if small else local,
        mesh=mesh,
        in_specs=placed,
        out_specs=(
            P(("groups", "expert", "dp", "node"), None),
            P(("groups", "expert"), "dp", None, None, "node"),
            P(("groups", "expert"), "dp", None, None, "node"),
            P(("groups", "expert"), "dp", "node"),
        ),
        check_vma=False,
    )
```

```python
import jax
import jax.numpy as jnp
from jax import lax
from jax.experimental import pallas as pl
from jax.experimental.pallas import tpu as pltpu
from jax.sharding import PartitionSpec as P


PAD = 80
TILE = 512


def whole_kernel(
    routes_ref, gates_ref, gout, gpre, upre, wdn, dg_ref, da_ref, du_ref, dw_out,
    meta_ref, a32, u32, tok, wv, rows, own, dhs, dhr, wall, acc, dwv, mb, rk, gt, scs, scr,
    loc, x_sem, m_send, m_recv, z_up, z_dn, z_recv, c_send, c_recv, d_send, d_recv,
    w_send, w_recv, s_send, s_recv, o_sem,
):
    half = wv.shape[0]
    cap, src = gpre.shape[0], gpre.shape[1]
    e = lax.axis_index("expert")
    x = lax.axis_index("dp")
    z, c = e // 2, e % 2
    ox = 1 - x
    sib = 2 * z + 1 - c
    hid = wv.shape[1]
    lanes = hid // 128

    def take(ref, s):
        return jnp.concatenate(
            [ref[h, pl.ds(s, cap, stride=src), :] for h in range(lanes)], axis=1
        )

    def put(ref, s, value):
        for h in range(lanes):
            ref[h, pl.ds(s, cap, stride=src), :] = value[:, h * 128:h * 128 + 128]

    def remote(src, dst, ss, rs, ee, xx):
        return pltpu.make_async_remote_copy(
            src_ref=src, dst_ref=dst, send_sem=ss, recv_sem=rs,
            device_id={"expert": ee, "dp": xx}, device_id_type=pl.DeviceIdType.MESH,
        )

    def order(k):
        inner = jnp.where(k == 0, 1, jnp.where(k == 1, 0, k))
        low = jnp.where((z == 1) | (z == 2), inner, k)
        return jnp.where(z < 2, low, 3 - low)

    mine = gout.at[:, pl.ds(pl.multiple_of(x * half, 128), half)]
    other = gout.at[:, pl.ds(pl.multiple_of(ox * half, 128), half)]
    tok_copy = pltpu.make_async_copy(mine, tok.at[e, 0], loc.at[0])
    w_copy = pltpu.make_async_copy(wdn.at[0], wv, loc.at[1])
    tok_copy.start()
    w_copy.start()
    barrier = pltpu.get_barrier_semaphore()
    peers = [((e + d) % 8, x, 0, e, (e + d) % 8) for d in range(1, 8)]
    peers += [((e + d) % 8, ox, 1, e + 8, (e + d) % 8 + 8) for d in range(8)]
    for ee, xx, _, _, _ in peers:
        pl.semaphore_signal(
            barrier, inc=1, device_id={"expert": ee, "dp": xx},
            device_id_type=pl.DeviceIdType.MESH,
        )
    meta_ref[0:4, :] = routes_ref[...].astype(jnp.float32)
    meta_ref[4:8, :] = gates_ref[...].astype(jnp.float32)
    mb[e] = meta_ref[...]
    wall[:, 0:2 * PAD, :] = jnp.zeros((4, 2 * PAD, hid), jnp.bfloat16)
    tok_copy.wait()
    pl.semaphore_wait(barrier, 15)

    def meta_copy(i):
        ee, xx, q, slot, _ = peers[i]
        return remote(meta_ref, mb.at[slot], m_send.at[i], m_recv.at[slot], ee, xx)

    for i in range(15):
        meta_copy(i).start()
    x_copy = remote(other, tok.at[e, 1], x_sem.at[0], x_sem.at[1], e, ox)
    x_copy.start()

    def up(zp, q):
        t = tok.at[2 * zp + c, q]
        return remote(t, t, z_up.at[zp, q], z_recv.at[zp, q], e + 2, x)

    def down(zp, q):
        t = tok.at[2 * zp + c, q]
        return remote(t, t, z_dn.at[zp, q], z_recv.at[zp, q], e - 2, x)

    def across(zp, q):
        t = tok.at[2 * zp + c, q]
        return remote(t, t, c_send.at[zp, q], c_recv.at[zp, q], sib, x)

    def arrived(zp, q):
        t = tok.at[2 * zp + c, q]
        remote(t, t, z_up.at[zp, q], z_recv.at[zp, q], e, ox).wait_recv()

    def sibling(zp, q):
        t = tok.at[2 * zp + 1 - c, q]
        remote(t, t, c_send.at[zp, q], c_recv.at[zp, q], sib, x).wait_recv()

    def forward(zp, q):
        @pl.when((zp <= z) & (z < 3))
        def _():
            up(zp, q).start()

        @pl.when((zp >= z) & (z > 0))
        def _():
            down(zp, q).start()

        across(zp, q).start()

    forward(z, 0)
    for h in range(lanes):
        at = slice(h * 128, h * 128 + 128)
        a32[h] = gpre[:, :, at].astype(jnp.float32).reshape(cap * src, 128)
        u32[h] = upre[:, :, at].astype(jnp.float32).reshape(cap * src, 128)

    for i in range(15):
        ee, xx, q, _, slot = peers[i]
        remote(meta_ref, mb.at[slot], m_send.at[i], m_recv.at[slot], ee, xx).wait_recv()

    named = (mb[:, 0:4, :] == e.astype(jnp.float32)).astype(jnp.float32)
    hit = jnp.sum(named, axis=1)
    gt[...] = jnp.sum(named * mb[:, 4:8, :], axis=1)
    before = (
        lax.broadcasted_iota(jnp.int32, (128, 128), 0)
        < lax.broadcasted_iota(jnp.int32, (128, 128), 1)
    )
    rank = jnp.dot(
        hit.astype(jnp.bfloat16), before.astype(jnp.float32).astype(jnp.bfloat16),
        preferred_element_type=jnp.float32,
    )
    rk[...] = jnp.where(hit > 0.5, rank, -1.0)
    slot_id = lax.broadcasted_iota(jnp.int32, (PAD, 128), 0).astype(jnp.float32)

    def placer(b):
        return (slot_id == rk[pl.ds(b, 1), :]).astype(jnp.float32)

    def w_copy_out(zp):
        return remote(
            wall.at[zp, 0:2 * PAD], wall.at[zp, 2 * PAD:4 * PAD],
            w_send.at[zp], w_recv.at[zp], e, ox,
        )

    @pl.loop(0, 4)
    def _(k):
        zp = order(k)
        for cc in range(2):
            s = 2 * zp + cc
            place = placer(s)
            gate = jnp.sum(place * gt[pl.ds(s, 1), :], axis=1, keepdims=True)[0:cap]
            a = take(a32, s)
            u = take(u32, s)
            wall[zp, cc * PAD:cc * PAD + cap, :] = (
                gate * (a * jax.nn.sigmoid(a) * u)
            ).astype(jnp.bfloat16)

    acc[...] = jnp.zeros_like(acc)
    x_copy.wait_recv()
    forward(z, 1)
    for k in range(4):
        w_copy_out(order(k)).start()
    w_copy.wait()

    def dh_copy(zp):
        return remote(dhs.at[zp], dhr.at[zp], d_send.at[zp], d_recv.at[zp], e, ox)

    def score_copy(s):
        return remote(scs.at[s], scr.at[e], s_send.at[s], s_recv.at[e], s, x)

    def finish(zp, last):
        w_copy_out(zp).wait_recv()

        @pl.loop(0, half // TILE)
        def _(t):
            at = pl.ds(pl.multiple_of(t * TILE, TILE), TILE)
            total = acc[at, :] + lax.dot_general(
                rows[:, at], wall[zp], (((0,), (0,)), ((), ())),
                preferred_element_type=jnp.float32,
            )
            if last:
                dwv[at, :] = total.astype(jnp.bfloat16)
                pltpu.make_async_copy(dwv.at[at, :], dw_out.at[0, at, :], o_sem.at[t]).start()
            else:
                acc[at, :] = total

        dh_copy(zp).wait_recv()
        for cc in range(2):
            s = 2 * zp + cc
            place = placer(s)
            gate = jnp.sum(place * gt[pl.ds(s, 1), :], axis=1, keepdims=True)[0:cap]
            a = take(a32, s)
            u = take(u32, s)
            dh = (own[cc] + dhr[zp, cc * PAD:(cc + 1) * PAD, :].astype(jnp.float32))
            dh = dh[0:cap]
            sig = jax.nn.sigmoid(a)
            act = a * sig
            score = jnp.sum(dh * (act * u), axis=1, keepdims=True)
            d_act = gate * dh
            put(a32, s, d_act * u * sig * (1.0 + a * (1.0 - sig)))
            put(u32, s, d_act * act)
            by_token = jnp.sum(place[0:cap] * score, axis=0, keepdims=True)
            full = jnp.broadcast_to(by_token, (8, 128))

            @pl.when(s == e)
            def _():
                scr[e] = full

            @pl.when(s != e)
            def _():
                scs[s] = full
                score_copy(s).start()

    def relay(d, q):
        @pl.when(z >= d)
        def _():
            arrived(z - d, q)
            forward(z - d, q)

        @pl.when(z + d < 4)
        def _():
            arrived(z + d, q)
            forward(z + d, q)

    @pl.loop(0, 4)
    def _(k):
        zp = order(k)
        end = (z == 0) | (z == 3)

        @pl.when(k == 0)
        def _():
            relay(1, 0)

        @pl.when(k == 1)
        def _():
            relay(1, 1)

        @pl.when(k == 2)
        def _():
            relay(2, 0)

        @pl.when((k == 3) & (z > 0) & (z < 3))
        def _():
            relay(2, 1)

        @pl.when(k > 0)
        def _():
            finish(order(k - 1), False)

        @pl.when((k == 2) & end)
        def _():
            relay(2, 1)

        @pl.when((k == 3) & end)
        def _():
            relay(3, 0)
            relay(3, 1)

        sibling(zp, 0)
        sibling(zp, 1)
        for q in (1, 0):
            for cc in range(2):
                s = 2 * zp + cc
                j = (q * 2 + cc) * PAD
                rows[j:j + PAD, :] = jnp.dot(
                    placer(q * 8 + s).astype(jnp.bfloat16), tok[s, q],
                    preferred_element_type=jnp.float32,
                ).astype(jnp.bfloat16)
            part = jnp.dot(
                rows[q * 2 * PAD:(q + 1) * 2 * PAD, :], wv[...],
                preferred_element_type=jnp.float32,
            )
            if q == 1:
                dhs[zp] = part.astype(jnp.bfloat16)
                dh_copy(zp).start()
            else:
                own[...] = part.reshape(2, PAD, hid)

    finish(order(3), True)
    for h in range(lanes):
        at = slice(h * 128, h * 128 + 128)
        da_ref[:, :, at] = a32[h].reshape(cap, src, 128).astype(jnp.bfloat16)
        du_ref[:, :, at] = u32[h].reshape(cap, src, 128).astype(jnp.bfloat16)

    for d in range(1, 8):
        s = (e + d) % 8
        remote(scs.at[s], scr.at[s], s_send.at[s], s_recv.at[s], s, x).wait_recv()
    routes = meta_ref[0:4, :]
    total = jnp.zeros((4, 128), jnp.float32)
    for i in range(8):
        total += jnp.where(routes == float(i), scr[i, 0:1, :], 0.0)
    dg_ref[...] = total

    x_copy.wait_send()
    for i in range(15):
        meta_copy(i).wait_send()
    for zp in range(4):
        for q in range(2):
            @pl.when((zp <= z) & (z < 3))
            def _():
                up(zp, q).wait_send()

            @pl.when((zp >= z) & (z > 0))
            def _():
                down(zp, q).wait_send()

            across(zp, q).wait_send()
        dh_copy(zp).wait_send()
        w_copy_out(zp).wait_send()
    for d in range(1, 8):
        score_copy((e + d) % 8).wait_send()
    for t in range(half // TILE):
        at = pl.ds(t * TILE, TILE)
        pltpu.make_async_copy(dwv.at[at, :], dw_out.at[0, at, :], o_sem.at[t]).wait()


def local_kernel(grad_out, routes, gates, gate_pre, up_pre, w_down):
    half, hid = w_down.shape[1], w_down.shape[2]
    cap, src = gate_pre.shape[3], gate_pre.shape[2]
    slots = (cap, src, hid)
    vmem = pl.BlockSpec(memory_space=pltpu.VMEM)
    hbm = pl.BlockSpec(memory_space=pl.ANY)
    dma = pltpu.SemaphoreType.DMA
    bf, f4 = jnp.bfloat16, jnp.float32
    dg, d_a, d_u, d_w = pl.pallas_call(
        whole_kernel,
        out_shape=(
            jax.ShapeDtypeStruct((4, 128), f4),
            jax.ShapeDtypeStruct(slots, bf),
            jax.ShapeDtypeStruct(slots, bf),
            jax.ShapeDtypeStruct(w_down.shape, bf),
        ),
        in_specs=[vmem, vmem, hbm, vmem, vmem, hbm],
        out_specs=(vmem, vmem, vmem, hbm),
        scratch_shapes=[
            pltpu.VMEM((8, 128), f4),
            pltpu.VMEM((hid // 128, cap * src, 128), f4),
            pltpu.VMEM((hid // 128, cap * src, 128), f4),
            pltpu.VMEM((8, 2, 128, half), bf),
            pltpu.VMEM((half, hid), bf),
            pltpu.VMEM((4 * PAD, half), bf),
            pltpu.VMEM((2, PAD, hid), f4),
            pltpu.VMEM((4, 2 * PAD, hid), bf),
            pltpu.VMEM((4, 2 * PAD, hid), bf),
            pltpu.VMEM((4, 4 * PAD, hid), bf),
            pltpu.VMEM((half, hid), f4),
            pltpu.VMEM((half, hid), bf),
            pltpu.VMEM((16, 8, 128), f4),
            pltpu.VMEM((16, 128), f4),
            pltpu.VMEM((16, 128), f4),
            pltpu.VMEM((8, 8, 128), f4),
            pltpu.VMEM((8, 8, 128), f4),
            dma((2,)), dma((2,)), dma((15,)), dma((16,)),
            dma((4, 2)), dma((4, 2)), dma((4, 2)), dma((4, 2)), dma((4, 2)),
            dma((4,)), dma((4,)), dma((4,)), dma((4,)),
            dma((8,)), dma((8,)), dma((half // TILE,)),
        ],
        compiler_params=pltpu.CompilerParams(
            collective_id=0, has_side_effects=True, vmem_limit_bytes=56 * 1024 * 1024
        ),
    )(
        routes.T, gates.T, grad_out,
        jnp.swapaxes(gate_pre[0, 0], 0, 1), jnp.swapaxes(up_pre[0, 0], 0, 1), w_down,
    )
    d_a, d_u = (jnp.swapaxes(v, 0, 1)[None, None] for v in (d_a, d_u))
    return (dg.T, d_a, d_u, d_w)


def local(grad_out, routes, gates, gate_pre, up_pre, w_down):
    tok_rows, width = grad_out.shape
    topk = routes.shape[1]
    sources = gate_pre.shape[2]
    capacity = gate_pre.shape[3]
    hidden = gate_pre.shape[4]
    experts = lax.axis_size("expert")
    node_count = lax.axis_size("node")
    count = tok_rows * topk
    slot_count = sources * capacity
    flat_routes = routes.reshape(count)
    member = (flat_routes[:, None] == jnp.arange(experts, dtype=jnp.int32)[None, :]).astype(
        jnp.int32
    )
    rank = jnp.sum(jnp.cumsum(member, axis=0) * member, axis=1) - 1
    slot_of = flat_routes * capacity + rank
    placer = jnp.arange(experts * capacity, dtype=jnp.int32)[:, None] == slot_of[None, :]
    placer_f = placer.astype(jnp.float32)
    by_token = jnp.sum(
        placer.reshape(experts * capacity, tok_rows, topk).astype(jnp.int32), axis=2
    ).astype(jnp.bfloat16)
    send_rows = (
        jnp.dot(by_token, grad_out, preferred_element_type=jnp.float32)
        .astype(jnp.bfloat16)
        .reshape(experts, capacity, width)
    )
    send_gates = (
        jnp.dot(placer_f, gates.reshape(count).astype(jnp.float32), precision=lax.Precision.HIGHEST)
        .astype(jnp.bfloat16)
        .reshape(experts, capacity)
    )
    pair_rows, pair_gates = (
        lax.all_gather(send_rows[None], "node", axis=0, tiled=True),
        lax.all_gather(send_gates[None], "node", axis=0, tiled=True),
    )
    recv_rows, recv_gates = (
        lax.all_to_all(pair_rows, "expert", split_axis=1, concat_axis=0, tiled=True),
        lax.all_to_all(pair_gates, "expert", split_axis=1, concat_axis=0, tiled=True),
    )
    rows = recv_rows.reshape(slot_count, width)
    gate_col = recv_gates.reshape(slot_count).astype(jnp.float32)
    pre_a = gate_pre.reshape(slot_count, hidden).astype(jnp.float32)
    pre_u = up_pre.reshape(slot_count, hidden).astype(jnp.float32)
    columns = rows
    grad_h = jnp.dot(
        columns,
        lax.all_gather(w_down, "dp", axis=1, tiled=True)[0],
        preferred_element_type=jnp.float32,
    )
    sig = jax.nn.sigmoid(pre_a)
    act = pre_a * sig
    hact = act * pre_u
    partial_score = jnp.sum(grad_h * hact, axis=1)
    d_act = gate_col[:, None] * grad_h
    d_a = (
        (d_act * pre_u * sig * (1.0 + pre_a * (1.0 - sig)))
        .astype(jnp.bfloat16)
        .reshape(gate_pre.shape)
    )
    d_u = (d_act * act).astype(jnp.bfloat16).reshape(up_pre.shape)
    weighted = (gate_col[:, None] * hact).astype(jnp.bfloat16)
    columns = rows
    grad_w = lax.psum_scatter(
        lax.dot_general(
            columns, weighted, (((0,), (0,)), ((), ())), preferred_element_type=jnp.float32
        ).astype(jnp.bfloat16),
        "dp",
        scatter_dimension=0,
        tiled=True,
    )
    d_w = grad_w[None]
    returned = lax.all_to_all(
        partial_score.reshape(sources, 1, capacity),
        ("expert", "node"),
        split_axis=0,
        concat_axis=1,
        tiled=True,
    )
    summed = jnp.sum(returned.reshape(experts, node_count, capacity), axis=1).reshape(
        experts * capacity
    )
    d_gates = jnp.dot(summed, placer_f, precision=lax.Precision.HIGHEST).reshape(tok_rows, topk)
    return (d_gates, d_a, d_u, d_w)


def solution(mesh):
    placed = (
        P(("groups", "expert", "dp", "node"), None),
        P(("groups", "expert", "dp", "node"), None),
        P(("groups", "expert", "dp", "node"), None),
        P(("groups", "expert"), "dp", None, None, "node"),
        P(("groups", "expert"), "dp", None, None, "node"),
        P("expert", "dp", "node"),
    )
    sizes = dict(mesh.shape)
    small = (sizes["expert"], sizes["dp"], sizes["node"]) == (8, 2, 1)
    return jax.shard_map(
        local_kernel if small else local,
        mesh=mesh,
        in_specs=placed,
        out_specs=(
            P(("groups", "expert", "dp", "node"), None),
            P(("groups", "expert"), "dp", None, None, "node"),
            P(("groups", "expert"), "dp", None, None, "node"),
            P(("groups", "expert"), "dp", "node"),
        ),
        check_vma=False,
    )
```

```python
import jax
import jax.numpy as jnp
from jax import lax
from jax.experimental import pallas as pl
from jax.experimental.pallas import tpu as pltpu
from jax.sharding import PartitionSpec as P


PAD = 80
TILE = 512


def whole_kernel(
    routes_ref, gates_ref, gout, gpre, upre, wdn, dg_ref, da_ref, du_ref, dw_out,
    meta_ref, a32, u32, tok, wv, rows, own, dhs, dhr, wall, acc, dwv, mb, rk, gt, scs, scr,
    loc, x_sem, m_send, m_recv, z_up, z_dn, z_recv, c_send, c_recv, d_send, d_recv,
    w_send, w_recv, s_send, s_recv, o_sem,
):
    half = wv.shape[0]
    cap, src = gpre.shape[0], gpre.shape[1]
    e = lax.axis_index("expert")
    x = lax.axis_index("dp")
    z, c = e // 2, e % 2
    ox = 1 - x
    sib = 2 * z + 1 - c
    hid = wv.shape[1]
    lanes = hid // 128

    def take(ref, s):
        return jnp.concatenate(
            [ref[h, pl.ds(s, cap, stride=src), :] for h in range(lanes)], axis=1
        )

    def put(ref, s, value):
        for h in range(lanes):
            ref[h, pl.ds(s, cap, stride=src), :] = value[:, h * 128:h * 128 + 128]

    def remote(src, dst, ss, rs, ee, xx):
        return pltpu.make_async_remote_copy(
            src_ref=src, dst_ref=dst, send_sem=ss, recv_sem=rs,
            device_id={"expert": ee, "dp": xx}, device_id_type=pl.DeviceIdType.MESH,
        )

    def order(k):
        inner = jnp.where(k == 0, 1, jnp.where(k == 1, 0, k))
        low = jnp.where((z == 1) | (z == 2), inner, k)
        return jnp.where(z < 2, low, 3 - low)

    mine = gout.at[:, pl.ds(pl.multiple_of(x * half, 128), half)]
    tok_copy = pltpu.make_async_copy(mine, tok.at[e, 0], loc.at[0])
    w_copy = pltpu.make_async_copy(wdn.at[0], wv, loc.at[1])
    tok_copy.start()
    w_copy.start()
    barrier = pltpu.get_barrier_semaphore()
    peers = [((e + d) % 8, x, 0, e, (e + d) % 8) for d in range(1, 8)]
    peers += [((e + d) % 8, ox, 1, e + 8, (e + d) % 8 + 8) for d in range(8)]
    for ee, xx, _, _, _ in peers:
        pl.semaphore_signal(
            barrier, inc=1, device_id={"expert": ee, "dp": xx},
            device_id_type=pl.DeviceIdType.MESH,
        )
    meta_ref[0:4, :] = routes_ref[...].astype(jnp.float32)
    meta_ref[4:8, :] = gates_ref[...].astype(jnp.float32)
    mb[e] = meta_ref[...]
    wall[:, 0:2 * PAD, :] = jnp.zeros((4, 2 * PAD, hid), jnp.bfloat16)
    tok_copy.wait()
    pl.semaphore_wait(barrier, 15)

    def meta_copy(i):
        ee, xx, q, slot, _ = peers[i]
        return remote(meta_ref, mb.at[slot], m_send.at[i], m_recv.at[slot], ee, xx)

    for i in range(15):
        meta_copy(i).start()
    part_w = half // 2

    def x_copy(r):
        src = gout.at[:, pl.ds(pl.multiple_of(ox * half + r * part_w, 128), part_w)]
        return remote(src, unit(e, 2 + r), x_sem.at[r], x_sem.at[2 + r], e, ox)

    def unit(s, r):
        return tok.at[s, r // 2, :, r % 2 * part_w:(r % 2 + 1) * part_w]

    x_copy(0).start()
    x_copy(1).start()

    def up(zp, q):
        t = unit(2 * zp + c, q)
        return remote(t, t, z_up.at[zp, q], z_recv.at[zp, q], e + 2, x)

    def down(zp, q):
        t = unit(2 * zp + c, q)
        return remote(t, t, z_dn.at[zp, q], z_recv.at[zp, q], e - 2, x)

    def across(zp, q):
        t = unit(2 * zp + c, q)
        return remote(t, t, c_send.at[zp, q], c_recv.at[zp, q], sib, x)

    def arrived(zp, q):
        t = unit(2 * zp + c, q)
        remote(t, t, z_up.at[zp, q], z_recv.at[zp, q], e, ox).wait_recv()

    def sibling(zp, q):
        t = unit(2 * zp + 1 - c, q)
        remote(t, t, c_send.at[zp, q], c_recv.at[zp, q], sib, x).wait_recv()

    def forward(zp, q):
        @pl.when((zp <= z) & (z < 3))
        def _():
            up(zp, q).start()

        @pl.when((zp >= z) & (z > 0))
        def _():
            down(zp, q).start()

        across(zp, q).start()

    forward(z, 0)
    forward(z, 1)
    for h in range(lanes):
        at = slice(h * 128, h * 128 + 128)
        a32[h] = gpre[:, :, at].astype(jnp.float32).reshape(cap * src, 128)
        u32[h] = upre[:, :, at].astype(jnp.float32).reshape(cap * src, 128)

    for i in range(15):
        ee, xx, q, _, slot = peers[i]
        remote(meta_ref, mb.at[slot], m_send.at[i], m_recv.at[slot], ee, xx).wait_recv()

    named = (mb[:, 0:4, :] == e.astype(jnp.float32)).astype(jnp.float32)
    hit = jnp.sum(named, axis=1)
    gt[...] = jnp.sum(named * mb[:, 4:8, :], axis=1)
    before = (
        lax.broadcasted_iota(jnp.int32, (128, 128), 0)
        < lax.broadcasted_iota(jnp.int32, (128, 128), 1)
    )
    rank = jnp.dot(
        hit.astype(jnp.bfloat16), before.astype(jnp.float32).astype(jnp.bfloat16),
        preferred_element_type=jnp.float32,
    )
    rk[...] = jnp.where(hit > 0.5, rank, -1.0)
    slot_id = lax.broadcasted_iota(jnp.int32, (PAD, 128), 0).astype(jnp.float32)

    def placer(b):
        return (slot_id == rk[pl.ds(b, 1), :]).astype(jnp.float32)

    def w_copy_out(zp):
        return remote(
            wall.at[zp, 0:2 * PAD], wall.at[zp, 2 * PAD:4 * PAD],
            w_send.at[zp], w_recv.at[zp], e, ox,
        )

    @pl.loop(0, 4)
    def _(k):
        zp = order(k)
        for cc in range(2):
            s = 2 * zp + cc
            place = placer(s)
            gate = jnp.sum(place * gt[pl.ds(s, 1), :], axis=1, keepdims=True)[0:cap]
            a = take(a32, s)
            u = take(u32, s)
            wall[zp, cc * PAD:cc * PAD + cap, :] = (
                gate * (a * jax.nn.sigmoid(a) * u)
            ).astype(jnp.bfloat16)

    acc[...] = jnp.zeros_like(acc)
    for r in range(2):
        x_copy(r).wait_recv()
        forward(z, 2 + r)
    for k in range(4):
        w_copy_out(order(k)).start()
    w_copy.wait()

    def dh_copy(zp):
        return remote(dhs.at[zp], dhr.at[zp], d_send.at[zp], d_recv.at[zp], e, ox)

    def score_copy(s):
        return remote(scs.at[s], scr.at[e], s_send.at[s], s_recv.at[e], s, x)

    def finish(zp, last):
        w_copy_out(zp).wait_recv()

        @pl.loop(0, half // TILE)
        def _(t):
            at = pl.ds(pl.multiple_of(t * TILE, TILE), TILE)
            total = acc[at, :] + lax.dot_general(
                rows[:, at], wall[zp], (((0,), (0,)), ((), ())),
                preferred_element_type=jnp.float32,
            )
            if last:
                dwv[at, :] = total.astype(jnp.bfloat16)
                pltpu.make_async_copy(dwv.at[at, :], dw_out.at[0, at, :], o_sem.at[t]).start()
            else:
                acc[at, :] = total

        dh_copy(zp).wait_recv()
        for cc in range(2):
            s = 2 * zp + cc
            place = placer(s)
            gate = jnp.sum(place * gt[pl.ds(s, 1), :], axis=1, keepdims=True)[0:cap]
            a = take(a32, s)
            u = take(u32, s)
            dh = (own[cc] + dhr[zp, cc * PAD:(cc + 1) * PAD, :].astype(jnp.float32))
            dh = dh[0:cap]
            sig = jax.nn.sigmoid(a)
            act = a * sig
            score = jnp.sum(dh * (act * u), axis=1, keepdims=True)
            d_act = gate * dh
            put(a32, s, d_act * u * sig * (1.0 + a * (1.0 - sig)))
            put(u32, s, d_act * act)
            by_token = jnp.sum(place[0:cap] * score, axis=0, keepdims=True)
            full = jnp.broadcast_to(by_token, (8, 128))

            @pl.when(s == e)
            def _():
                scr[e] = full

            @pl.when(s != e)
            def _():
                scs[s] = full
                score_copy(s).start()

    def relay(d, q):
        @pl.when(z >= d)
        def _():
            arrived(z - d, q)
            forward(z - d, q)

        @pl.when(z + d < 4)
        def _():
            arrived(z + d, q)
            forward(z + d, q)

    @pl.loop(0, 4)
    def _(k):
        zp = order(k)
        end = (z == 0) | (z == 3)

        @pl.when(k == 0)
        def _():
            relay(1, 0)
            relay(1, 1)

        @pl.when(k == 1)
        def _():
            relay(1, 2)
            relay(1, 3)

        @pl.when(k == 2)
        def _():
            relay(2, 0)

        @pl.when((k == 3) & (z > 0) & (z < 3))
        def _():
            relay(2, 2)
            relay(2, 3)
            relay(2, 1)

        @pl.when(k > 0)
        def _():
            finish(order(k - 1), False)

        @pl.when((k == 2) & end)
        def _():
            relay(2, 2)
            relay(2, 3)
            relay(2, 1)

        @pl.when((k == 3) & end)
        def _():
            relay(3, 0)
            relay(3, 2)
            relay(3, 3)

        for q in (1, 0):
            if q == 0:
                @pl.when((k == 3) & end)
                def _():
                    relay(3, 1)

            sibling(zp, 2 * q)
            sibling(zp, 2 * q + 1)
            for cc in range(2):
                s = 2 * zp + cc
                j = (q * 2 + cc) * PAD
                rows[j:j + PAD, :] = jnp.dot(
                    placer(q * 8 + s).astype(jnp.bfloat16), tok[s, q],
                    preferred_element_type=jnp.float32,
                ).astype(jnp.bfloat16)
            part = jnp.dot(
                rows[q * 2 * PAD:(q + 1) * 2 * PAD, :], wv[...],
                preferred_element_type=jnp.float32,
            )
            if q == 1:
                dhs[zp] = part.astype(jnp.bfloat16)
                dh_copy(zp).start()
            else:
                own[...] = part.reshape(2, PAD, hid)

    finish(order(3), True)
    for h in range(lanes):
        at = slice(h * 128, h * 128 + 128)
        da_ref[:, :, at] = a32[h].reshape(cap, src, 128).astype(jnp.bfloat16)
        du_ref[:, :, at] = u32[h].reshape(cap, src, 128).astype(jnp.bfloat16)

    for d in range(1, 8):
        s = (e + d) % 8
        remote(scs.at[s], scr.at[s], s_send.at[s], s_recv.at[s], s, x).wait_recv()
    routes = meta_ref[0:4, :]
    total = jnp.zeros((4, 128), jnp.float32)
    for i in range(8):
        total += jnp.where(routes == float(i), scr[i, 0:1, :], 0.0)
    dg_ref[...] = total

    x_copy(0).wait_send()
    x_copy(1).wait_send()
    for i in range(15):
        meta_copy(i).wait_send()
    for zp in range(4):
        for q in range(4):
            @pl.when((zp <= z) & (z < 3))
            def _():
                up(zp, q).wait_send()

            @pl.when((zp >= z) & (z > 0))
            def _():
                down(zp, q).wait_send()

            across(zp, q).wait_send()
        dh_copy(zp).wait_send()
        w_copy_out(zp).wait_send()
    for d in range(1, 8):
        score_copy((e + d) % 8).wait_send()
    for t in range(half // TILE):
        at = pl.ds(t * TILE, TILE)
        pltpu.make_async_copy(dwv.at[at, :], dw_out.at[0, at, :], o_sem.at[t]).wait()


def local_kernel(grad_out, routes, gates, gate_pre, up_pre, w_down):
    half, hid = w_down.shape[1], w_down.shape[2]
    cap, src = gate_pre.shape[3], gate_pre.shape[2]
    slots = (cap, src, hid)
    vmem = pl.BlockSpec(memory_space=pltpu.VMEM)
    hbm = pl.BlockSpec(memory_space=pl.ANY)
    dma = pltpu.SemaphoreType.DMA
    bf, f4 = jnp.bfloat16, jnp.float32
    dg, d_a, d_u, d_w = pl.pallas_call(
        whole_kernel,
        out_shape=(
            jax.ShapeDtypeStruct((4, 128), f4),
            jax.ShapeDtypeStruct(slots, bf),
            jax.ShapeDtypeStruct(slots, bf),
            jax.ShapeDtypeStruct(w_down.shape, bf),
        ),
        in_specs=[vmem, vmem, hbm, vmem, vmem, hbm],
        out_specs=(vmem, vmem, vmem, hbm),
        scratch_shapes=[
            pltpu.VMEM((8, 128), f4),
            pltpu.VMEM((hid // 128, cap * src, 128), f4),
            pltpu.VMEM((hid // 128, cap * src, 128), f4),
            pltpu.VMEM((8, 2, 128, half), bf),
            pltpu.VMEM((half, hid), bf),
            pltpu.VMEM((4 * PAD, half), bf),
            pltpu.VMEM((2, PAD, hid), f4),
            pltpu.VMEM((4, 2 * PAD, hid), bf),
            pltpu.VMEM((4, 2 * PAD, hid), bf),
            pltpu.VMEM((4, 4 * PAD, hid), bf),
            pltpu.VMEM((half, hid), f4),
            pltpu.VMEM((half, hid), bf),
            pltpu.VMEM((16, 8, 128), f4),
            pltpu.VMEM((16, 128), f4),
            pltpu.VMEM((16, 128), f4),
            pltpu.VMEM((8, 8, 128), f4),
            pltpu.VMEM((8, 8, 128), f4),
            dma((2,)), dma((4,)), dma((15,)), dma((16,)),
            dma((4, 4)), dma((4, 4)), dma((4, 4)), dma((4, 4)), dma((4, 4)),
            dma((4,)), dma((4,)), dma((4,)), dma((4,)),
            dma((8,)), dma((8,)), dma((half // TILE,)),
        ],
        compiler_params=pltpu.CompilerParams(
            collective_id=0, has_side_effects=True, vmem_limit_bytes=56 * 1024 * 1024
        ),
    )(
        routes.T, gates.T, grad_out,
        jnp.swapaxes(gate_pre[0, 0], 0, 1), jnp.swapaxes(up_pre[0, 0], 0, 1), w_down,
    )
    d_a, d_u = (jnp.swapaxes(v, 0, 1)[None, None] for v in (d_a, d_u))
    return (dg.T, d_a, d_u, d_w)


def local(grad_out, routes, gates, gate_pre, up_pre, w_down):
    tok_rows, width = grad_out.shape
    topk = routes.shape[1]
    sources = gate_pre.shape[2]
    capacity = gate_pre.shape[3]
    hidden = gate_pre.shape[4]
    experts = lax.axis_size("expert")
    node_count = lax.axis_size("node")
    count = tok_rows * topk
    slot_count = sources * capacity
    flat_routes = routes.reshape(count)
    member = (flat_routes[:, None] == jnp.arange(experts, dtype=jnp.int32)[None, :]).astype(
        jnp.int32
    )
    rank = jnp.sum(jnp.cumsum(member, axis=0) * member, axis=1) - 1
    slot_of = flat_routes * capacity + rank
    placer = jnp.arange(experts * capacity, dtype=jnp.int32)[:, None] == slot_of[None, :]
    placer_f = placer.astype(jnp.float32)
    by_token = jnp.sum(
        placer.reshape(experts * capacity, tok_rows, topk).astype(jnp.int32), axis=2
    ).astype(jnp.bfloat16)
    send_rows = (
        jnp.dot(by_token, grad_out, preferred_element_type=jnp.float32)
        .astype(jnp.bfloat16)
        .reshape(experts, capacity, width)
    )
    send_gates = (
        jnp.dot(placer_f, gates.reshape(count).astype(jnp.float32), precision=lax.Precision.HIGHEST)
        .astype(jnp.bfloat16)
        .reshape(experts, capacity)
    )
    pair_rows, pair_gates = (
        lax.all_gather(send_rows[None], "node", axis=0, tiled=True),
        lax.all_gather(send_gates[None], "node", axis=0, tiled=True),
    )
    recv_rows, recv_gates = (
        lax.all_to_all(pair_rows, "expert", split_axis=1, concat_axis=0, tiled=True),
        lax.all_to_all(pair_gates, "expert", split_axis=1, concat_axis=0, tiled=True),
    )
    rows = recv_rows.reshape(slot_count, width)
    gate_col = recv_gates.reshape(slot_count).astype(jnp.float32)
    pre_a = gate_pre.reshape(slot_count, hidden).astype(jnp.float32)
    pre_u = up_pre.reshape(slot_count, hidden).astype(jnp.float32)
    columns = rows
    grad_h = jnp.dot(
        columns,
        lax.all_gather(w_down, "dp", axis=1, tiled=True)[0],
        preferred_element_type=jnp.float32,
    )
    sig = jax.nn.sigmoid(pre_a)
    act = pre_a * sig
    hact = act * pre_u
    partial_score = jnp.sum(grad_h * hact, axis=1)
    d_act = gate_col[:, None] * grad_h
    d_a = (
        (d_act * pre_u * sig * (1.0 + pre_a * (1.0 - sig)))
        .astype(jnp.bfloat16)
        .reshape(gate_pre.shape)
    )
    d_u = (d_act * act).astype(jnp.bfloat16).reshape(up_pre.shape)
    weighted = (gate_col[:, None] * hact).astype(jnp.bfloat16)
    columns = rows
    grad_w = lax.psum_scatter(
        lax.dot_general(
            columns, weighted, (((0,), (0,)), ((), ())), preferred_element_type=jnp.float32
        ).astype(jnp.bfloat16),
        "dp",
        scatter_dimension=0,
        tiled=True,
    )
    d_w = grad_w[None]
    returned = lax.all_to_all(
        partial_score.reshape(sources, 1, capacity),
        ("expert", "node"),
        split_axis=0,
        concat_axis=1,
        tiled=True,
    )
    summed = jnp.sum(returned.reshape(experts, node_count, capacity), axis=1).reshape(
        experts * capacity
    )
    d_gates = jnp.dot(summed, placer_f, precision=lax.Precision.HIGHEST).reshape(tok_rows, topk)
    return (d_gates, d_a, d_u, d_w)


def solution(mesh):
    placed = (
        P(("groups", "expert", "dp", "node"), None),
        P(("groups", "expert", "dp", "node"), None),
        P(("groups", "expert", "dp", "node"), None),
        P(("groups", "expert"), "dp", None, None, "node"),
        P(("groups", "expert"), "dp", None, None, "node"),
        P("expert", "dp", "node"),
    )
    sizes = dict(mesh.shape)
    small = (sizes["expert"], sizes["dp"], sizes["node"]) == (8, 2, 1)
    return jax.shard_map(
        local_kernel if small else local,
        mesh=mesh,
        in_specs=placed,
        out_specs=(
            P(("groups", "expert", "dp", "node"), None),
            P(("groups", "expert"), "dp", None, None, "node"),
            P(("groups", "expert"), "dp", None, None, "node"),
            P(("groups", "expert"), "dp", "node"),
        ),
        check_vma=False,
    )
```

```python
import jax
import jax.numpy as jnp
from jax import lax
from jax.experimental import pallas as pl
from jax.experimental.pallas import tpu as pltpu
from jax.sharding import PartitionSpec as P


PAD = 80
TILE = 512


def whole_kernel(
    routes_ref, gates_ref, gout, gpre_hbm, upre_hbm, wdn, dg_ref, da_ref, du_ref, dw_out,
    gpre, upre, meta_ref, a32, u32, tok, wv, rows, own, dhs, dhr, wall, acc, dwv, mb, rk, gt, scs, scr,
    loc, x_sem, m_send, m_recv, z_up, z_dn, z_recv, c_send, c_recv, d_send, d_recv,
    w_send, w_recv, s_send, s_recv, o_sem,
):
    half = wv.shape[0]
    cap, src = gpre.shape[0], gpre.shape[1]
    e = lax.axis_index("expert")
    x = lax.axis_index("dp")
    z, c = e // 2, e % 2
    ox = 1 - x
    sib = 2 * z + 1 - c
    hid = wv.shape[1]
    lanes = hid // 128

    def take(ref, s):
        return jnp.concatenate(
            [ref[h, pl.ds(s, cap, stride=src), :] for h in range(lanes)], axis=1
        )

    def put(ref, s, value):
        for h in range(lanes):
            ref[h, pl.ds(s, cap, stride=src), :] = value[:, h * 128:h * 128 + 128]

    def remote(src, dst, ss, rs, ee, xx):
        return pltpu.make_async_remote_copy(
            src_ref=src, dst_ref=dst, send_sem=ss, recv_sem=rs,
            device_id={"expert": ee, "dp": xx}, device_id_type=pl.DeviceIdType.MESH,
        )

    def order(k):
        inner = jnp.where(k == 0, 1, jnp.where(k == 1, 0, k))
        low = jnp.where((z == 1) | (z == 2), inner, k)
        return jnp.where(z < 2, low, 3 - low)

    mine = gout.at[:, pl.ds(pl.multiple_of(x * half, 128), half)]
    tok_copy = pltpu.make_async_copy(mine, tok.at[e, 0], loc.at[0])
    w_copy = pltpu.make_async_copy(wdn.at[0], wv, loc.at[1])
    tok_copy.start()
    w_copy.start()
    g_copy = pltpu.make_async_copy(gpre_hbm, gpre, loc.at[2])
    u_copy = pltpu.make_async_copy(upre_hbm, upre, loc.at[3])
    g_copy.start()
    u_copy.start()
    barrier = pltpu.get_barrier_semaphore()
    peers = [((e + d) % 8, x, 0, e, (e + d) % 8) for d in range(1, 8)]
    peers += [((e + d) % 8, ox, 1, e + 8, (e + d) % 8 + 8) for d in range(8)]
    for ee, xx, _, _, _ in peers:
        pl.semaphore_signal(
            barrier, inc=1, device_id={"expert": ee, "dp": xx},
            device_id_type=pl.DeviceIdType.MESH,
        )
    meta_ref[0:4, :] = routes_ref[...].astype(jnp.float32)
    meta_ref[4:8, :] = gates_ref[...].astype(jnp.float32)
    mb[e] = meta_ref[...]
    wall[:, 0:2 * PAD, :] = jnp.zeros((4, 2 * PAD, hid), jnp.bfloat16)
    tok_copy.wait()
    pl.semaphore_wait(barrier, 15)

    def meta_copy(i):
        ee, xx, q, slot, _ = peers[i]
        return remote(meta_ref, mb.at[slot], m_send.at[i], m_recv.at[slot], ee, xx)

    for i in range(15):
        meta_copy(i).start()
    part_w = half // 2

    def x_copy(r):
        src = gout.at[:, pl.ds(pl.multiple_of(ox * half + r * part_w, 128), part_w)]
        return remote(src, unit(e, 2 + r), x_sem.at[r], x_sem.at[2 + r], e, ox)

    def unit(s, r):
        return tok.at[s, r // 2, :, r % 2 * part_w:(r % 2 + 1) * part_w]

    x_copy(0).start()
    x_copy(1).start()

    def up(zp, q):
        t = unit(2 * zp + c, q)
        return remote(t, t, z_up.at[zp, q], z_recv.at[zp, q], e + 2, x)

    def down(zp, q):
        t = unit(2 * zp + c, q)
        return remote(t, t, z_dn.at[zp, q], z_recv.at[zp, q], e - 2, x)

    def across(zp, q):
        t = unit(2 * zp + c, q)
        return remote(t, t, c_send.at[zp, q], c_recv.at[zp, q], sib, x)

    def arrived(zp, q):
        t = unit(2 * zp + c, q)
        remote(t, t, z_up.at[zp, q], z_recv.at[zp, q], e, ox).wait_recv()

    def sibling(zp, q):
        t = unit(2 * zp + 1 - c, q)
        remote(t, t, c_send.at[zp, q], c_recv.at[zp, q], sib, x).wait_recv()

    def forward(zp, q):
        @pl.when((zp <= z) & (z < 3))
        def _():
            up(zp, q).start()

        @pl.when((zp >= z) & (z > 0))
        def _():
            down(zp, q).start()

        across(zp, q).start()

    forward(z, 0)
    forward(z, 1)
    g_copy.wait()
    u_copy.wait()
    for h in range(lanes):
        at = slice(h * 128, h * 128 + 128)
        a32[h] = gpre[:, :, at].astype(jnp.float32).reshape(cap * src, 128)
        u32[h] = upre[:, :, at].astype(jnp.float32).reshape(cap * src, 128)

    for i in range(15):
        ee, xx, q, _, slot = peers[i]
        remote(meta_ref, mb.at[slot], m_send.at[i], m_recv.at[slot], ee, xx).wait_recv()

    named = (mb[:, 0:4, :] == e.astype(jnp.float32)).astype(jnp.float32)
    hit = jnp.sum(named, axis=1)
    gt[...] = jnp.sum(named * mb[:, 4:8, :], axis=1)
    before = (
        lax.broadcasted_iota(jnp.int32, (128, 128), 0)
        < lax.broadcasted_iota(jnp.int32, (128, 128), 1)
    )
    rank = jnp.dot(
        hit.astype(jnp.bfloat16), before.astype(jnp.float32).astype(jnp.bfloat16),
        preferred_element_type=jnp.float32,
    )
    rk[...] = jnp.where(hit > 0.5, rank, -1.0)
    slot_id = lax.broadcasted_iota(jnp.int32, (PAD, 128), 0).astype(jnp.float32)

    def placer(b):
        return (slot_id == rk[pl.ds(b, 1), :]).astype(jnp.float32)

    def w_copy_out(zp):
        return remote(
            wall.at[zp, 0:2 * PAD], wall.at[zp, 2 * PAD:4 * PAD],
            w_send.at[zp], w_recv.at[zp], e, ox,
        )

    @pl.loop(0, 4)
    def _(k):
        zp = order(k)
        for cc in range(2):
            s = 2 * zp + cc
            place = placer(s)
            gate = jnp.sum(place * gt[pl.ds(s, 1), :], axis=1, keepdims=True)[0:cap]
            a = take(a32, s)
            u = take(u32, s)
            wall[zp, cc * PAD:cc * PAD + cap, :] = (
                gate * (a * jax.nn.sigmoid(a) * u)
            ).astype(jnp.bfloat16)

    acc[...] = jnp.zeros_like(acc)
    for r in range(2):
        x_copy(r).wait_recv()
        forward(z, 2 + r)
    for k in range(4):
        w_copy_out(order(k)).start()
    w_copy.wait()

    def dh_copy(zp):
        return remote(dhs.at[zp], dhr.at[zp], d_send.at[zp], d_recv.at[zp], e, ox)

    def score_copy(s):
        return remote(scs.at[s], scr.at[e], s_send.at[s], s_recv.at[e], s, x)

    def finish(zp, last):
        w_copy_out(zp).wait_recv()

        @pl.loop(0, half // TILE)
        def _(t):
            at = pl.ds(pl.multiple_of(t * TILE, TILE), TILE)
            total = acc[at, :] + lax.dot_general(
                rows[:, at], wall[zp], (((0,), (0,)), ((), ())),
                preferred_element_type=jnp.float32,
            )
            if last:
                dwv[at, :] = total.astype(jnp.bfloat16)
                pltpu.make_async_copy(dwv.at[at, :], dw_out.at[0, at, :], o_sem.at[t]).start()
            else:
                acc[at, :] = total

        dh_copy(zp).wait_recv()
        for cc in range(2):
            s = 2 * zp + cc
            place = placer(s)
            gate = jnp.sum(place * gt[pl.ds(s, 1), :], axis=1, keepdims=True)[0:cap]
            a = take(a32, s)
            u = take(u32, s)
            dh = (own[cc] + dhr[zp, cc * PAD:(cc + 1) * PAD, :].astype(jnp.float32))
            dh = dh[0:cap]
            sig = jax.nn.sigmoid(a)
            act = a * sig
            score = jnp.sum(dh * (act * u), axis=1, keepdims=True)
            d_act = gate * dh
            put(a32, s, d_act * u * sig * (1.0 + a * (1.0 - sig)))
            put(u32, s, d_act * act)
            by_token = jnp.sum(place[0:cap] * score, axis=0, keepdims=True)
            full = jnp.broadcast_to(by_token, (8, 128))

            @pl.when(s == e)
            def _():
                scr[e] = full

            @pl.when(s != e)
            def _():
                scs[s] = full
                score_copy(s).start()

    def relay(d, q):
        @pl.when(z >= d)
        def _():
            arrived(z - d, q)
            forward(z - d, q)

        @pl.when(z + d < 4)
        def _():
            arrived(z + d, q)
            forward(z + d, q)

    @pl.loop(0, 4)
    def _(k):
        zp = order(k)
        end = (z == 0) | (z == 3)

        @pl.when(k == 0)
        def _():
            relay(1, 0)
            relay(1, 1)

        @pl.when(k == 1)
        def _():
            relay(1, 2)
            relay(1, 3)

        @pl.when(k == 2)
        def _():
            relay(2, 0)

        @pl.when((k == 3) & (z > 0) & (z < 3))
        def _():
            relay(2, 2)
            relay(2, 3)
            relay(2, 1)

        @pl.when(k > 0)
        def _():
            finish(order(k - 1), False)

        @pl.when((k == 2) & end)
        def _():
            relay(2, 2)
            relay(2, 3)
            relay(2, 1)

        @pl.when((k == 3) & end)
        def _():
            relay(3, 0)
            relay(3, 2)
            relay(3, 3)

        for q in (1, 0):
            if q == 0:
                @pl.when((k == 3) & end)
                def _():
                    relay(3, 1)

            sibling(zp, 2 * q)
            sibling(zp, 2 * q + 1)
            for cc in range(2):
                s = 2 * zp + cc
                j = (q * 2 + cc) * PAD
                rows[j:j + PAD, :] = jnp.dot(
                    placer(q * 8 + s).astype(jnp.bfloat16), tok[s, q],
                    preferred_element_type=jnp.float32,
                ).astype(jnp.bfloat16)
            part = jnp.dot(
                rows[q * 2 * PAD:(q + 1) * 2 * PAD, :], wv[...],
                preferred_element_type=jnp.float32,
            )
            if q == 1:
                dhs[zp] = part.astype(jnp.bfloat16)
                dh_copy(zp).start()
            else:
                own[...] = part.reshape(2, PAD, hid)

    finish(order(3), True)
    for h in range(lanes):
        at = slice(h * 128, h * 128 + 128)
        da_ref[:, :, at] = a32[h].reshape(cap, src, 128).astype(jnp.bfloat16)
        du_ref[:, :, at] = u32[h].reshape(cap, src, 128).astype(jnp.bfloat16)

    for d in range(1, 8):
        s = (e + d) % 8
        remote(scs.at[s], scr.at[s], s_send.at[s], s_recv.at[s], s, x).wait_recv()
    routes = meta_ref[0:4, :]
    total = jnp.zeros((4, 128), jnp.float32)
    for i in range(8):
        total += jnp.where(routes == float(i), scr[i, 0:1, :], 0.0)
    dg_ref[...] = total

    x_copy(0).wait_send()
    x_copy(1).wait_send()
    for i in range(15):
        meta_copy(i).wait_send()
    for zp in range(4):
        for q in range(4):
            @pl.when((zp <= z) & (z < 3))
            def _():
                up(zp, q).wait_send()

            @pl.when((zp >= z) & (z > 0))
            def _():
                down(zp, q).wait_send()

            across(zp, q).wait_send()
        dh_copy(zp).wait_send()
        w_copy_out(zp).wait_send()
    for d in range(1, 8):
        score_copy((e + d) % 8).wait_send()
    for t in range(half // TILE):
        at = pl.ds(t * TILE, TILE)
        pltpu.make_async_copy(dwv.at[at, :], dw_out.at[0, at, :], o_sem.at[t]).wait()


def place_kernel(dg, d_a, d_u, d_w, dg_out, da_out, du_out, dw_out):
    dg_out[...] = dg[...]
    da_out[...] = d_a[...]
    du_out[...] = d_u[...]
    dw_out[...] = d_w[...]


def local_kernel(grad_out, routes, gates, gate_pre, up_pre, w_down):
    half, hid = w_down.shape[1], w_down.shape[2]
    cap, src = gate_pre.shape[3], gate_pre.shape[2]
    slots = (cap, src, hid)
    vmem = pl.BlockSpec(memory_space=pltpu.VMEM)
    hbm = pl.BlockSpec(memory_space=pl.ANY)
    dma = pltpu.SemaphoreType.DMA
    bf, f4 = jnp.bfloat16, jnp.float32
    dg, d_a, d_u, d_w = pl.pallas_call(
        whole_kernel,
        out_shape=(
            jax.ShapeDtypeStruct((4, 128), f4),
            jax.ShapeDtypeStruct(slots, bf),
            jax.ShapeDtypeStruct(slots, bf),
            jax.ShapeDtypeStruct(w_down.shape, bf),
        ),
        in_specs=[vmem, vmem, hbm, hbm, hbm, hbm],
        out_specs=(vmem, vmem, vmem, hbm),
        scratch_shapes=[
            pltpu.VMEM(slots, bf),
            pltpu.VMEM(slots, bf),
            pltpu.VMEM((8, 128), f4),
            pltpu.VMEM((hid // 128, cap * src, 128), f4),
            pltpu.VMEM((hid // 128, cap * src, 128), f4),
            pltpu.VMEM((8, 2, 128, half), bf),
            pltpu.VMEM((half, hid), bf),
            pltpu.VMEM((4 * PAD, half), bf),
            pltpu.VMEM((2, PAD, hid), f4),
            pltpu.VMEM((4, 2 * PAD, hid), bf),
            pltpu.VMEM((4, 2 * PAD, hid), bf),
            pltpu.VMEM((4, 4 * PAD, hid), bf),
            pltpu.VMEM((half, hid), f4),
            pltpu.VMEM((half, hid), bf),
            pltpu.VMEM((16, 8, 128), f4),
            pltpu.VMEM((16, 128), f4),
            pltpu.VMEM((16, 128), f4),
            pltpu.VMEM((8, 8, 128), f4),
            pltpu.VMEM((8, 8, 128), f4),
            dma((4,)), dma((4,)), dma((15,)), dma((16,)),
            dma((4, 4)), dma((4, 4)), dma((4, 4)), dma((4, 4)), dma((4, 4)),
            dma((4,)), dma((4,)), dma((4,)), dma((4,)),
            dma((8,)), dma((8,)), dma((half // TILE,)),
        ],
        compiler_params=pltpu.CompilerParams(
            collective_id=0, has_side_effects=True, vmem_limit_bytes=56 * 1024 * 1024
        ),
    )(
        routes.T, gates.T, grad_out,
        jnp.swapaxes(gate_pre[0, 0], 0, 1), jnp.swapaxes(up_pre[0, 0], 0, 1), w_down,
    )
    steps = 4
    specs = (
        pl.BlockSpec((4, 128), lambda i: (0, 0)),
        pl.BlockSpec((cap // steps, src, hid), lambda i: (i, 0, 0)),
        pl.BlockSpec((cap // steps, src, hid), lambda i: (i, 0, 0)),
        pl.BlockSpec((1, half // steps, hid), lambda i: (0, i, 0)),
    )
    dg, d_a, d_u, d_w = pl.pallas_call(
        place_kernel,
        grid=(steps,),
        out_shape=tuple(jax.ShapeDtypeStruct(v.shape, v.dtype) for v in (dg, d_a, d_u, d_w)),
        in_specs=specs,
        out_specs=specs,
        compiler_params=pltpu.CompilerParams(vmem_limit_bytes=60 * 1024 * 1024),
    )(dg, d_a, d_u, d_w)
    d_a, d_u = (jnp.swapaxes(v, 0, 1)[None, None] for v in (d_a, d_u))
    return (dg.T, d_a, d_u, d_w)


def local(grad_out, routes, gates, gate_pre, up_pre, w_down):
    tok_rows, width = grad_out.shape
    topk = routes.shape[1]
    sources = gate_pre.shape[2]
    capacity = gate_pre.shape[3]
    hidden = gate_pre.shape[4]
    experts = lax.axis_size("expert")
    node_count = lax.axis_size("node")
    count = tok_rows * topk
    slot_count = sources * capacity
    flat_routes = routes.reshape(count)
    member = (flat_routes[:, None] == jnp.arange(experts, dtype=jnp.int32)[None, :]).astype(
        jnp.int32
    )
    rank = jnp.sum(jnp.cumsum(member, axis=0) * member, axis=1) - 1
    slot_of = flat_routes * capacity + rank
    placer = jnp.arange(experts * capacity, dtype=jnp.int32)[:, None] == slot_of[None, :]
    placer_f = placer.astype(jnp.float32)
    by_token = jnp.sum(
        placer.reshape(experts * capacity, tok_rows, topk).astype(jnp.int32), axis=2
    ).astype(jnp.bfloat16)
    send_rows = (
        jnp.dot(by_token, grad_out, preferred_element_type=jnp.float32)
        .astype(jnp.bfloat16)
        .reshape(experts, capacity, width)
    )
    send_gates = (
        jnp.dot(placer_f, gates.reshape(count).astype(jnp.float32), precision=lax.Precision.HIGHEST)
        .astype(jnp.bfloat16)
        .reshape(experts, capacity)
    )
    pair_rows, pair_gates = (
        lax.all_gather(send_rows[None], "node", axis=0, tiled=True),
        lax.all_gather(send_gates[None], "node", axis=0, tiled=True),
    )
    recv_rows, recv_gates = (
        lax.all_to_all(pair_rows, "expert", split_axis=1, concat_axis=0, tiled=True),
        lax.all_to_all(pair_gates, "expert", split_axis=1, concat_axis=0, tiled=True),
    )
    rows = recv_rows.reshape(slot_count, width)
    gate_col = recv_gates.reshape(slot_count).astype(jnp.float32)
    pre_a = gate_pre.reshape(slot_count, hidden).astype(jnp.float32)
    pre_u = up_pre.reshape(slot_count, hidden).astype(jnp.float32)
    columns = rows
    grad_h = jnp.dot(
        columns,
        lax.all_gather(w_down, "dp", axis=1, tiled=True)[0],
        preferred_element_type=jnp.float32,
    )
    sig = jax.nn.sigmoid(pre_a)
    act = pre_a * sig
    hact = act * pre_u
    partial_score = jnp.sum(grad_h * hact, axis=1)
    d_act = gate_col[:, None] * grad_h
    d_a = (
        (d_act * pre_u * sig * (1.0 + pre_a * (1.0 - sig)))
        .astype(jnp.bfloat16)
        .reshape(gate_pre.shape)
    )
    d_u = (d_act * act).astype(jnp.bfloat16).reshape(up_pre.shape)
    weighted = (gate_col[:, None] * hact).astype(jnp.bfloat16)
    columns = rows
    grad_w = lax.psum_scatter(
        lax.dot_general(
            columns, weighted, (((0,), (0,)), ((), ())), preferred_element_type=jnp.float32
        ).astype(jnp.bfloat16),
        "dp",
        scatter_dimension=0,
        tiled=True,
    )
    d_w = grad_w[None]
    returned = lax.all_to_all(
        partial_score.reshape(sources, 1, capacity),
        ("expert", "node"),
        split_axis=0,
        concat_axis=1,
        tiled=True,
    )
    summed = jnp.sum(returned.reshape(experts, node_count, capacity), axis=1).reshape(
        experts * capacity
    )
    d_gates = jnp.dot(summed, placer_f, precision=lax.Precision.HIGHEST).reshape(tok_rows, topk)
    return (d_gates, d_a, d_u, d_w)


def solution(mesh):
    placed = (
        P(("groups", "expert", "dp", "node"), None),
        P(("groups", "expert", "dp", "node"), None),
        P(("groups", "expert", "dp", "node"), None),
        P(("groups", "expert"), "dp", None, None, "node"),
        P(("groups", "expert"), "dp", None, None, "node"),
        P("expert", "dp", "node"),
    )
    sizes = dict(mesh.shape)
    small = (sizes["expert"], sizes["dp"], sizes["node"]) == (8, 2, 1)
    return jax.shard_map(
        local_kernel if small else local,
        mesh=mesh,
        in_specs=placed,
        out_specs=(
            P(("groups", "expert", "dp", "node"), None),
            P(("groups", "expert"), "dp", None, None, "node"),
            P(("groups", "expert"), "dp", None, None, "node"),
            P(("groups", "expert"), "dp", "node"),
        ),
        check_vma=False,
    )
```
